32 devices in a mesh: groups: 2 (over y), sector: 4 (over z), op: 4 (over x, core).
Axes of the slice: x: 2, y: 2, z: 4, core: 2. Of those that a mesh axis runs over, the one named last changes fastest.
Arguments:
- states: bfloat16 [4, 4, 4, 64, 128], P('groups', 'sector'), parts along dimension 0, may hold values from -6 to 6
- left_ops: bfloat16 [16, 8, 64, 64], P('op', ('groups', 'sector')), parts along dimension 1, may hold values from -3 to 3
- right_ops: bfloat16 [16, 8, 128, 128], P('op', ('groups', 'sector')), parts along dimension 1, may hold values from -3 to 3
- rows_live: int32 [8], P('groups'), parts along dimension 0, may hold values from 32 to 64
- cols_live: int32 [8], P('groups'), parts along dimension 0, may hold values from 64 to 128
- block_live: int32 [8, 4], P('groups'), parts along dimension 0, may hold values 0 or 1
Outputs:
- sigma_out: bfloat16 [4, 4, 4, 64, 128], P('groups', 'op', 'sector'), parts along dimension 0
- rayleigh: float32 [4, 2], P('groups'), parts along dimension 0
- correlation: float32 [4, 2], P('groups'), parts along dimension 0
The draws below stay inside these ranges and needn't reach their ends.
There are 2 independent parts, one for each index of `groups`. The reference program is written for one: setup_inputs(seed, part) draws one part's arguments, and reference() takes and returns one part's arrays. A program takes and returns all parts, laid end to end along the dimension named above; each array names one. Nothing has to cross between parts.
All inputs are finite; a program needn't handle non-finite values.
Results may differ from the reference program's by a relative error of at most 0.0052.
Values may be sent and summed in bfloat16 or wider, within the bound.
A program may use at most 64 MiB of HBM per device.

```python
import math
import jax
import jax.numpy as jnp
from jax import lax

RB = 64
CB = 128
NV = 2
NA = 4
NB = 4
K = 16


def diagonal_part(key, terms, sectors, width):
    sign_key, size_key = jax.random.split(key, 2)
    signs = (jax.random.randint(sign_key, (terms, sectors, 1, 1), 0, 2) * 2 - 1).astype(jnp.float32)
    magnitude = jax.random.uniform(size_key, (terms, sectors, 1, 1), minval=0.5, maxval=1.5)
    return signs * magnitude * jnp.eye(width, dtype=jnp.float32)


def draw_left_ops(key, part):
    key = jax.random.fold_in(key, 11)
    diag_key, noise_key = jax.random.split(key, 2)
    noise = jnp.clip(jax.random.normal(noise_key, (K, NA, RB, RB)), -4.0, 4.0)
    blocks = diagonal_part(diag_key, K, NA, RB) + noise * (0.6 / math.sqrt(RB))
    return blocks.astype(jnp.bfloat16)


def draw_right_ops(key, part):
    key = jax.random.fold_in(key, 12)
    diag_key, noise_key = jax.random.split(key, 2)
    noise = jnp.clip(jax.random.normal(noise_key, (K, NB, CB, CB)), -4.0, 4.0)
    blocks = diagonal_part(diag_key, K, NB, CB) + noise * (0.6 / math.sqrt(CB))
    return blocks.astype(jnp.bfloat16)


def set_ends(result, rng, smallest, high):
    dims = result.shape
    index_at = [jax.random.randint(jax.random.fold_in(rng, axis), (), 0, dims[axis]) for axis in range(len(dims))]
    result = result.at[tuple(index_at)].set(smallest)
    longest = dims.index(max(dims))
    index_at[longest] = (index_at[longest] + 1) % dims[longest]
    return result.at[tuple(index_at)].set(high)


def steps_of(key, dims, pieces, smallest, high):
    def one(dim, shards_of):
        heights = jax.random.uniform(jax.random.fold_in(jax.random.fold_in(key, 6), dim), (shards_of,), jnp.float32, smallest / len(pieces), high / len(pieces))
        return jnp.repeat(jnp.exp(heights), dims[dim] // shards_of).reshape((-1,) + (1,) * (len(dims) - dim - 1))

    loudness = one(*pieces[0])
    for cut in pieces[1:]:
        loudness = loudness * one(*cut)
    return loudness


def normal_values(own_key, extent, scale, limit, cuts=(), kind=jnp.bfloat16):
    loudness = steps_of(own_key, extent, cuts, -0.22, 0.18) if cuts else 1.0
    values = jax.random.normal(own_key, extent, jnp.float32) * scale * loudness
    return jnp.minimum(jnp.maximum(values, -limit), limit).astype(kind)


def setup_inputs(seed: int = 0, part: int = 0) -> dict:
    key_list = jax.random.split(jax.random.key(seed), 7)
    own_keys = jax.random.split(jax.random.fold_in(key_list[6], part), 7)
    states = normal_values(own_keys[0], (NV, NA, NB, RB, CB), 1.0, 6.0, ((1, 4),))
    left_ops = draw_left_ops(jax.random.fold_in(jax.random.fold_in(key_list[6], part), 71), part)
    right_ops = draw_right_ops(jax.random.fold_in(jax.random.fold_in(key_list[6], part), 71), part)
    rows_live = set_ends(jax.random.randint(own_keys[3], (NA,), RB // 2, RB + 1), jax.random.fold_in(own_keys[3], 1), RB // 2, RB).astype(jnp.int32)
    cols_live = set_ends(jax.random.randint(own_keys[4], (NB,), CB // 2, CB + 1), jax.random.fold_in(own_keys[4], 1), CB // 2, CB).astype(jnp.int32)
    block_live = set_ends((jax.random.randint(own_keys[5], (NA, NB), 0, 3) < 2).astype(jnp.int32), jax.random.fold_in(own_keys[5], 1), 0, 1)
    return dict(states=states, left_ops=left_ops, right_ops=right_ops, rows_live=rows_live, cols_live=cols_live, block_live=block_live)


def reference(states, left_ops, right_ops, rows_live, cols_live, block_live):
    row_ok = jnp.arange(RB)[None, :] < rows_live[:, None]
    col_ok = jnp.arange(CB)[None, :] < cols_live[:, None]
    right_wide = right_ops.astype(jnp.float32)

    def one_sector(inputs):
        sector_states, sector_ops, sector_rows, sector_blocks = inputs
        live_mask = (sector_blocks[:, None, None] == 1) & sector_rows[None, :, None] & col_ok[:, None, :]
        masked = jnp.where(live_mask[None], sector_states, jnp.zeros_like(sector_states))
        masked_wide = masked.astype(jnp.float32)
        left_done = jnp.einsum('kxy,vbyz->kvbxz', sector_ops.astype(jnp.float32), masked_wide).astype(jnp.bfloat16)
        total_sigma = jnp.einsum('kvbxy,kbzy->vbxz', left_done.astype(jnp.float32), right_wide)
        total_sigma = jnp.where(live_mask[None], total_sigma, jnp.float32(0.0))
        ray_part = jnp.einsum('vbxy,wbxy->vw', masked_wide, total_sigma, precision=lax.Precision.HIGHEST)
        over_part = jnp.einsum('vbxy,wbxy->vw', masked, masked, preferred_element_type=jnp.float32)
        return total_sigma.astype(jnp.bfloat16), ray_part, over_part

    sigma_all, ray_all, over_all = lax.map(one_sector, (jnp.moveaxis(states, 1, 0), jnp.moveaxis(left_ops, 1, 0), row_ok, block_live))
    norm_scale = jnp.float32(1.0 / (NA * NB * RB * CB))
    sigma_out = jnp.moveaxis(sigma_all, 0, 1)
    rayleigh = jnp.sum(ray_all, axis=0) * norm_scale
    correlation = jnp.sum(over_all, axis=0) * norm_scale
    return sigma_out, rayleigh, correlation
```

```python
import functools

import jax
import jax.numpy as jnp
from jax import lax
from jax.experimental import pallas as pl
from jax.experimental.pallas import tpu as pltpu
from jax.sharding import PartitionSpec as P

MESH = pl.DeviceIdType.MESH


def each(count, body):
    if count <= 16:
        for i in range(count):
            body(i)
    else:
        lax.fori_loop(0, count, lambda i, c: (body(i), c)[1], 0)


def kernel(
    n, ops, norm,
    rows_ref, cols_ref, blocks_ref, states_ref, left_ref, right_ref,
    sigma_ref, ray_ref, corr_ref,
    left_own, left_send_buf, left_all, right_all, states_all, stats,
    local_sem, left_ss, left_rs, right_ss, right_rs, st_ss, st_rs, stat_ss, stat_rs,
):
    s = lax.axis_index("sector")
    o = lax.axis_index("op")
    share = states_all.shape[0]
    kl = left_own.shape[0]
    rows, width = states_all.shape[2:]
    owner = s // share
    slot = lax.rem(s, share)
    mate = o + 1 - 2 * lax.rem(o, 2)

    load_left = pltpu.make_async_copy(left_ref.at[:, 0], left_own, local_sem.at[0])
    load_left.start()
    load_right = pltpu.make_async_copy(right_ref.at[:, 0], right_all.at[o], local_sem.at[1])
    load_right.start()
    load_states = pltpu.make_async_copy(
        states_ref.at[:, 0, s], states_all.at[slot], local_sem.at[2]
    )

    @pl.when(owner == o)
    def _():
        load_states.start()

    barrier = pltpu.get_barrier_semaphore()

    def greet(r):
        pl.semaphore_signal(
            barrier,
            inc=1,
            device_id={
                "sector": lax.rem(s + (r + 1) // ops, n),
                "op": lax.rem(o + lax.rem(r + 1, ops), ops),
            },
            device_id_type=MESH,
        )

    each(n * ops - 1, greet)

    load_left.wait()
    packed = [
        jnp.concatenate([left_own[2 * j], left_own[2 * j + 1]], axis=1) for j in range(kl // 2)
    ]
    for j in range(kl // 2):
        left_send_buf[j] = packed[j]

    @pl.when(owner == o)
    def _():
        for j in range(kl // 2):
            left_all[slot, o, j] = packed[j]

    pl.semaphore_wait(barrier, n * ops - 1)

    def right_copy(origin, src, to, sem):
        return pltpu.make_async_remote_copy(
            src_ref=src,
            dst_ref=right_all.at[origin],
            send_sem=right_ss.at[sem],
            recv_sem=right_rs.at[origin],
            device_id={"op": to},
            device_id_type=MESH,
        )

    far = [lax.rem(o + 2 * p, ops) for p in range(1, ops // 2)]
    own_right = right_ref.at[:, 0]
    sends = [right_copy(o, own_right, far[p], p) for p in range(len(far))]
    sends.append(right_copy(o, own_right, mate, len(far)))
    for copy in sends:
        copy.start()

    def left_copy(d):
        return pltpu.make_async_remote_copy(
            src_ref=left_send_buf,
            dst_ref=left_all.at[slot, o],
            send_sem=left_ss.at[d],
            recv_sem=left_rs.at[slot, o],
            device_id={"sector": lax.rem(s + d, n), "op": owner},
            device_id_type=MESH,
        )

    def state_copy(d):
        to = lax.rem(s + d, n)
        return pltpu.make_async_remote_copy(
            src_ref=states_ref.at[:, 0, to],
            dst_ref=states_all.at[slot],
            send_sem=st_ss.at[d],
            recv_sem=st_rs.at[slot],
            device_id={"sector": to, "op": o},
            device_id_type=MESH,
        )

    @pl.when(owner == o)
    def _():
        each(n - 1, lambda d: state_copy(d + 1).start())

    each(n - 1, lambda d: left_copy(d + 1).start())

    @pl.when(owner != o)
    def _():
        left_copy(0).start()

    for p in range(len(far)):
        origin = far[p]
        right_copy(origin, right_all.at[origin], mate, len(far) + 1 + p).wait_recv()
        copy = right_copy(origin, right_all.at[origin], mate, len(far) + 1 + p)
        copy.start()
        sends.append(copy)

    load_right.wait()

    @pl.when(owner == o)
    def _():
        load_states.wait()

    row_at = lax.broadcasted_iota(jnp.int32, (rows, width), 0)
    col_at = lax.broadcasted_iota(jnp.int32, (rows, width), 1)
    zero = jnp.zeros((rows, width), jnp.bfloat16)
    totals = [jnp.zeros((1, width), jnp.float32) for _ in range(8)]

    def one_block(i, totals, first):
        a = o * share + i

        @pl.when(a != s)
        def _():
            state_copy_in(i).wait_recv()

        live = (
            (row_at < rows_ref[a]) & (col_at < cols_ref[s]) & (blocks_ref[a, s] == 1)
        )
        masked = [
            jnp.where(live, states_all[i, v].astype(jnp.float32), 0.0) for v in range(2)
        ]
        narrow = [m.astype(jnp.bfloat16) for m in masked]
        pairs = [
            jnp.concatenate(
                [
                    jnp.concatenate([m, zero], axis=1),
                    jnp.concatenate([zero, m], axis=1),
                ],
                axis=0,
            )
            for m in narrow
        ]
        acc = jnp.zeros((2 * rows, width), jnp.float32)
        for step in range(ops):
            if step == 0:
                g = o
            elif step == 1:
                g = mate
            elif step % 2 == 0:
                g = far[step // 2 - 1]
            else:
                f = far[step // 2 - 1]
                g = f + 1 - 2 * lax.rem(f, 2)

            @pl.when(jnp.logical_or(a != s, g != o))
            def _():
                left_copy_in(i, g).wait_recv()

            if first and step % 2 == 1:
                right_copy(g, right_all.at[g], mate, 0).wait_recv()
            lhs = left_all[i, g].reshape(kl // 2 * rows, 2 * rows)
            done = []
            for v in range(2):
                t = jnp.dot(lhs, pairs[v], preferred_element_type=jnp.float32)
                t = t.astype(jnp.bfloat16)
                done.append(
                    jnp.concatenate(
                        [t[j * rows:(j + 1) * rows] for j in range(kl // 2)], axis=1
                    )
                )
            rhs = jnp.concatenate([right_all[g, k] for k in range(kl)], axis=1)
            acc += lax.dot_general(
                jnp.concatenate(done, axis=0), rhs, (((1,), (1,)), ((), ())),
                preferred_element_type=jnp.float32,
            )
        summed = [
            jnp.where(live, acc[v * rows:(v + 1) * rows], 0.0) for v in range(2)
        ]
        for v in range(2):
            sigma_ref[v, i, 0] = summed[v].astype(jnp.bfloat16)
        out = []
        for right in (summed, masked):
            for v in range(2):
                for w in range(2):
                    out.append(jnp.sum(masked[v] * right[w], axis=0, keepdims=True))
        return [x + y for x, y in zip(totals, out)]

    def state_copy_in(i):
        return pltpu.make_async_remote_copy(
            src_ref=states_ref.at[:, 0, s],
            dst_ref=states_all.at[i],
            send_sem=st_ss.at[0],
            recv_sem=st_rs.at[i],
            device_id={"sector": lax.rem(s + 1, n), "op": o},
            device_id_type=MESH,
        )

    def left_copy_in(i, g):
        return pltpu.make_async_remote_copy(
            src_ref=left_send_buf,
            dst_ref=left_all.at[i, g],
            send_sem=left_ss.at[0],
            recv_sem=left_rs.at[i, g],
            device_id={"sector": lax.rem(s + 1, n), "op": o},
            device_id_type=MESH,
        )

    totals = one_block(0, totals, True)
    if share > 1:
        totals = lax.fori_loop(
            1, share, lambda i, t: tuple(one_block(i, list(t), False)), tuple(totals)
        )

    rank = s * ops + o
    stats[rank] = jnp.concatenate(list(totals), axis=0)

    def tell(r):
        pltpu.make_async_remote_copy(
            src_ref=stats.at[rank],
            dst_ref=stats.at[rank],
            send_sem=stat_ss,
            recv_sem=stat_rs,
            device_id={
                "sector": lax.rem(s + (r + 1) // ops, n),
                "op": lax.rem(o + lax.rem(r + 1, ops), ops),
            },
            device_id_type=MESH,
        ).start()

    each(n * ops - 1, tell)

    for copy in sends:
        copy.wait_send()

    @pl.when(owner == o)
    def _():
        each(n - 1, lambda d: state_copy(d + 1).wait_send())

    each(n - 1, lambda d: left_copy(d + 1).wait_send())

    @pl.when(owner != o)
    def _():
        left_copy(0).wait_send()

    others = stats.at[pl.ds(0, n * ops - 1)]
    both = pltpu.make_async_remote_copy(
        src_ref=others, dst_ref=others, send_sem=stat_ss, recv_sem=stat_rs,
        device_id={"sector": lax.rem(s + 1, n), "op": o}, device_id_type=MESH,
    )
    both.wait_recv()
    both.wait_send()
    result = jnp.sum(jnp.sum(stats[...], axis=0), axis=1, keepdims=True) * norm
    for v in range(2):
        for w in range(2):
            at = 2 * v + w
            ray_ref[v:v + 1, w:w + 1] = result[at:at + 1]
            corr_ref[v:v + 1, w:w + 1] = result[4 + at:5 + at]


def on_device(mesh, states, left_ops, right_ops, rows_live, cols_live, block_live):
    n = mesh.shape["sector"]
    ops = mesh.shape["op"]
    kl, _, rows, _ = left_ops.shape
    width = right_ops.shape[2]
    nv = states.shape[0]
    left_sectors, right_sectors = block_live.shape
    share = left_sectors // ops
    assert nv == 2 and kl % 2 == 0 and ops % 2 == 0
    assert left_ops.shape[1] == 1 and right_ops.shape[1] == 1 and states.shape[1] == 1
    norm = 1.0 / (left_sectors * right_sectors * rows * width)
    smem = pl.BlockSpec(memory_space=pltpu.SMEM)
    vmem = pl.BlockSpec(memory_space=pltpu.VMEM)
    anywhere = pl.BlockSpec(memory_space=pl.ANY)
    dma = pltpu.SemaphoreType.DMA
    flops = 2 * nv * share * ops * kl * rows * width * (rows + width)
    return pl.pallas_call(
        functools.partial(kernel, n, ops, norm),
        out_shape=(
            jax.ShapeDtypeStruct((nv, share, 1, rows, width), jnp.bfloat16),
            jax.ShapeDtypeStruct((nv, nv), jnp.float32),
            jax.ShapeDtypeStruct((nv, nv), jnp.float32),
        ),
        in_specs=[smem, smem, smem, anywhere, anywhere, anywhere],
        out_specs=(vmem, vmem, vmem),
        scratch_shapes=[
            pltpu.VMEM((kl, rows, rows), jnp.bfloat16),
            pltpu.VMEM((kl // 2, rows, 2 * rows), jnp.bfloat16),
            pltpu.VMEM((share, ops, kl // 2, rows, 2 * rows), jnp.bfloat16),
            pltpu.VMEM((ops, kl, width, width), jnp.bfloat16),
            pltpu.VMEM((share, nv, rows, width), jnp.bfloat16),
            pltpu.VMEM((n * ops, 8, width), jnp.float32),
            dma((3,)),
            dma((n,)),
            dma((share, ops)),
            dma((ops,)),
            dma((ops,)),
            dma((n,)),
            dma((share,)),
            dma,
            dma,
        ],
        compiler_params=pltpu.CompilerParams(
            collective_id=0, has_side_effects=True, vmem_limit_bytes=48 * 1024 * 1024
        ),
        cost_estimate=pl.CostEstimate(
            flops=flops, bytes_accessed=1 << 20, transcendentals=0
        ),
    )(rows_live, cols_live, block_live, states, left_ops, right_ops)


def solution(mesh):
    placed = (
        P("groups", "sector", None, None, None),
        P("op", ("groups", "sector"), None, None),
        P("op", ("groups", "sector"), None, None),
        P("groups"),
        P("groups"),
        P("groups", None),
    )
    return jax.shard_map(
        functools.partial(on_device, mesh),
        mesh=mesh,
        in_specs=placed,
        out_specs=(P("groups", "op", "sector", None, None), P("groups", None), P("groups", None)),
        check_vma=False,
    )
```

```python
import functools

import jax
import jax.numpy as jnp
from jax import lax
from jax.experimental import pallas as pl
from jax.experimental.pallas import tpu as pltpu
from jax.sharding import PartitionSpec as P

MESH = pl.DeviceIdType.MESH


def each(count, body):
    if count <= 16:
        for i in range(count):
            body(i)
    else:
        lax.fori_loop(0, count, lambda i, c: (body(i), c)[1], 0)


def kernel(
    n, ops, norm,
    rows_hbm, cols_hbm, blocks_hbm, states_ref, left_ref, right_ref,
    sigma_out, ray_out, corr_out,
    sigma_ref, ray_ref, corr_ref,
    rows_ref, cols_ref, blocks_ref,
    left_own, left_send_buf, left_all, right_all, states_all, stats,
    local_sem, left_ss, left_rs, right_ss, right_rs, st_ss, st_rs, stat_ss, stat_rs,
):
    s = lax.axis_index("sector")
    o = lax.axis_index("op")
    share = states_all.shape[0]
    kl = left_own.shape[0]
    rows, width = states_all.shape[2:]
    owner = s // share
    slot = lax.rem(s, share)
    mate = o + 1 - 2 * lax.rem(o, 2)

    load_left = pltpu.make_async_copy(left_ref.at[:, 0], left_own, local_sem.at[0])
    load_left.start()
    load_right = pltpu.make_async_copy(right_ref.at[:, 0], right_all.at[o], local_sem.at[1])
    load_right.start()
    load_states = pltpu.make_async_copy(
        states_ref.at[:, 0, s], states_all.at[slot], local_sem.at[2]
    )

    @pl.when(owner == o)
    def _():
        load_states.start()

    tables = [
        pltpu.make_async_copy(src, dst, local_sem.at[3 + i])
        for i, (src, dst) in enumerate(
            [(rows_hbm, rows_ref), (cols_hbm, cols_ref), (blocks_hbm, blocks_ref)]
        )
    ]
    for copy in tables:
        copy.start()

    barrier = pltpu.get_barrier_semaphore()

    def greet(r):
        pl.semaphore_signal(
            barrier,
            inc=1,
            device_id={
                "sector": lax.rem(s + (r + 1) // ops, n),
                "op": lax.rem(o + lax.rem(r + 1, ops), ops),
            },
            device_id_type=MESH,
        )

    each(n * ops - 1, greet)

    load_left.wait()
    packed = [
        jnp.concatenate([left_own[2 * j], left_own[2 * j + 1]], axis=1) for j in range(kl // 2)
    ]
    for j in range(kl // 2):
        left_send_buf[j] = packed[j]

    @pl.when(owner == o)
    def _():
        for j in range(kl // 2):
            left_all[slot, o, j] = packed[j]

    pl.semaphore_wait(barrier, n * ops - 1)

    def right_copy(origin, src, to, sem):
        return pltpu.make_async_remote_copy(
            src_ref=src,
            dst_ref=right_all.at[origin],
            send_sem=right_ss.at[sem],
            recv_sem=right_rs.at[origin],
            device_id={"op": to},
            device_id_type=MESH,
        )

    far = [lax.rem(o + 2 * p, ops) for p in range(1, ops // 2)]
    own_right = right_ref.at[:, 0]
    sends = [right_copy(o, own_right, far[p], p) for p in range(len(far))]
    sends.append(right_copy(o, own_right, mate, len(far)))
    for copy in sends:
        copy.start()

    def left_copy(d):
        return pltpu.make_async_remote_copy(
            src_ref=left_send_buf,
            dst_ref=left_all.at[slot, o],
            send_sem=left_ss.at[d],
            recv_sem=left_rs.at[slot, o],
            device_id={"sector": lax.rem(s + d, n), "op": owner},
            device_id_type=MESH,
        )

    def state_copy(d):
        to = lax.rem(s + d, n)
        return pltpu.make_async_remote_copy(
            src_ref=states_ref.at[:, 0, to],
            dst_ref=states_all.at[slot],
            send_sem=st_ss.at[d],
            recv_sem=st_rs.at[slot],
            device_id={"sector": to, "op": o},
            device_id_type=MESH,
        )

    @pl.when(owner == o)
    def _():
        each(n - 1, lambda d: state_copy(d + 1).start())

    each(n - 1, lambda d: left_copy(d + 1).start())

    @pl.when(owner != o)
    def _():
        left_copy(0).start()

    for p in range(len(far)):
        origin = far[p]
        right_copy(origin, right_all.at[origin], mate, len(far) + 1 + p).wait_recv()
        copy = right_copy(origin, right_all.at[origin], mate, len(far) + 1 + p)
        copy.start()
        sends.append(copy)

    load_right.wait()
    for copy in tables:
        copy.wait()

    @pl.when(owner == o)
    def _():
        load_states.wait()

    row_at = lax.broadcasted_iota(jnp.int32, (rows, width), 0)
    col_at = lax.broadcasted_iota(jnp.int32, (rows, width), 1)
    zero = jnp.zeros((rows, width), jnp.bfloat16)
    totals = [jnp.zeros((1, width), jnp.float32) for _ in range(8)]

    def one_block(i, totals, first):
        a = o * share + i

        @pl.when(a != s)
        def _():
            state_copy_in(i).wait_recv()

        live = (
            (row_at < rows_ref[a]) & (col_at < cols_ref[s]) & (blocks_ref[a, s] == 1)
        )
        masked = [
            jnp.where(live, states_all[i, v].astype(jnp.float32), 0.0) for v in range(2)
        ]
        narrow = [m.astype(jnp.bfloat16) for m in masked]
        pairs = [
            jnp.concatenate(
                [
                    jnp.concatenate([m, zero], axis=1),
                    jnp.concatenate([zero, m], axis=1),
                ],
                axis=0,
            )
            for m in narrow
        ]
        acc = jnp.zeros((2 * rows, width), jnp.float32)
        for step in range(ops):
            if step == 0:
                g = o
            elif step == 1:
                g = mate
            elif step % 2 == 0:
                g = far[step // 2 - 1]
            else:
                f = far[step // 2 - 1]
                g = f + 1 - 2 * lax.rem(f, 2)

            @pl.when(jnp.logical_or(a != s, g != o))
            def _():
                left_copy_in(i, g).wait_recv()

            if first and step % 2 == 1:
                right_copy(g, right_all.at[g], mate, 0).wait_recv()
            lhs = left_all[i, g].reshape(kl // 2 * rows, 2 * rows)
            done = []
            for v in range(2):
                t = jnp.dot(lhs, pairs[v], preferred_element_type=jnp.float32)
                t = t.astype(jnp.bfloat16)
                done.append(
                    jnp.concatenate(
                        [t[j * rows:(j + 1) * rows] for j in range(kl // 2)], axis=1
                    )
                )
            rhs = jnp.concatenate([right_all[g, k] for k in range(kl)], axis=1)
            acc += lax.dot_general(
                jnp.concatenate(done, axis=0), rhs, (((1,), (1,)), ((), ())),
                preferred_element_type=jnp.float32,
            )
        summed = [
            jnp.where(live, acc[v * rows:(v + 1) * rows], 0.0) for v in range(2)
        ]
        for v in range(2):
            sigma_ref[v, i, 0] = summed[v].astype(jnp.bfloat16)
        out = []
        for right in (summed, masked):
            for v in range(2):
                for w in range(2):
                    out.append(jnp.sum(masked[v] * right[w], axis=0, keepdims=True))
        return [x + y for x, y in zip(totals, out)]

    def state_copy_in(i):
        return pltpu.make_async_remote_copy(
            src_ref=states_ref.at[:, 0, s],
            dst_ref=states_all.at[i],
            send_sem=st_ss.at[0],
            recv_sem=st_rs.at[i],
            device_id={"sector": lax.rem(s + 1, n), "op": o},
            device_id_type=MESH,
        )

    def left_copy_in(i, g):
        return pltpu.make_async_remote_copy(
            src_ref=left_send_buf,
            dst_ref=left_all.at[i, g],
            send_sem=left_ss.at[0],
            recv_sem=left_rs.at[i, g],
            device_id={"sector": lax.rem(s + 1, n), "op": o},
            device_id_type=MESH,
        )

    totals = one_block(0, totals, True)
    if share > 1:
        totals = lax.fori_loop(
            1, share, lambda i, t: tuple(one_block(i, list(t), False)), tuple(totals)
        )

    outs = [
        pltpu.make_async_copy(src, dst, local_sem.at[6 + i])
        for i, (src, dst) in enumerate(
            [(sigma_ref, sigma_out), (ray_ref, ray_out), (corr_ref, corr_out)]
        )
    ]
    outs[0].start()

    rank = s * ops + o
    stats[rank] = jnp.concatenate(list(totals), axis=0)

    def tell(r):
        pltpu.make_async_remote_copy(
            src_ref=stats.at[rank],
            dst_ref=stats.at[rank],
            send_sem=stat_ss,
            recv_sem=stat_rs,
            device_id={
                "sector": lax.rem(s + (r + 1) // ops, n),
                "op": lax.rem(o + lax.rem(r + 1, ops), ops),
            },
            device_id_type=MESH,
        ).start()

    each(n * ops - 1, tell)

    for copy in sends:
        copy.wait_send()

    @pl.when(owner == o)
    def _():
        each(n - 1, lambda d: state_copy(d + 1).wait_send())

    each(n - 1, lambda d: left_copy(d + 1).wait_send())

    @pl.when(owner != o)
    def _():
        left_copy(0).wait_send()

    others = stats.at[pl.ds(0, n * ops - 1)]
    both = pltpu.make_async_remote_copy(
        src_ref=others, dst_ref=others, send_sem=stat_ss, recv_sem=stat_rs,
        device_id={"sector": lax.rem(s + 1, n), "op": o}, device_id_type=MESH,
    )
    both.wait_recv()
    both.wait_send()
    result = jnp.sum(jnp.sum(stats[...], axis=0), axis=1, keepdims=True) * norm
    for v in range(2):
        for w in range(2):
            at = 2 * v + w
            ray_ref[v:v + 1, w:w + 1] = result[at:at + 1]
            corr_ref[v:v + 1, w:w + 1] = result[4 + at:5 + at]
    for copy in outs[1:]:
        copy.start()
    for copy in outs:
        copy.wait()


def write_out(a, b, c, a_out, b_out, c_out, sem):
    copies = [
        pltpu.make_async_copy(src, dst, sem.at[i])
        for i, (src, dst) in enumerate([(a, a_out), (b, b_out), (c, c_out)])
    ]
    for copy in copies:
        copy.start()
    for copy in copies:
        copy.wait()


def on_device(mesh, states, left_ops, right_ops, rows_live, cols_live, block_live):
    n = mesh.shape["sector"]
    ops = mesh.shape["op"]
    kl, _, rows, _ = left_ops.shape
    width = right_ops.shape[2]
    nv = states.shape[0]
    left_sectors, right_sectors = block_live.shape
    share = left_sectors // ops
    assert nv == 2 and kl % 2 == 0 and ops % 2 == 0
    assert left_ops.shape[1] == 1 and right_ops.shape[1] == 1 and states.shape[1] == 1
    norm = 1.0 / (left_sectors * right_sectors * rows * width)
    hbm = pl.BlockSpec(memory_space=pltpu.HBM)
    dma = pltpu.SemaphoreType.DMA
    flops = 2 * nv * share * ops * kl * rows * width * (rows + width)
    results = pl.pallas_call(
        functools.partial(kernel, n, ops, norm),
        out_shape=(
            jax.ShapeDtypeStruct((nv, share, 1, rows, width), jnp.bfloat16),
            jax.ShapeDtypeStruct((nv, nv), jnp.float32),
            jax.ShapeDtypeStruct((nv, nv), jnp.float32),
        ),
        in_specs=[hbm] * 6,
        out_specs=(hbm,) * 3,
        scratch_shapes=[
            pltpu.VMEM((nv, share, 1, rows, width), jnp.bfloat16),
            pltpu.VMEM((nv, nv), jnp.float32),
            pltpu.VMEM((nv, nv), jnp.float32),
            pltpu.SMEM(rows_live.shape, jnp.int32),
            pltpu.SMEM(cols_live.shape, jnp.int32),
            pltpu.SMEM(block_live.shape, jnp.int32),
            pltpu.VMEM((kl, rows, rows), jnp.bfloat16),
            pltpu.VMEM((kl // 2, rows, 2 * rows), jnp.bfloat16),
            pltpu.VMEM((share, ops, kl // 2, rows, 2 * rows), jnp.bfloat16),
            pltpu.VMEM((ops, kl, width, width), jnp.bfloat16),
            pltpu.VMEM((share, nv, rows, width), jnp.bfloat16),
            pltpu.VMEM((n * ops, 8, width), jnp.float32),
            dma((9,)),
            dma((n,)),
            dma((share, ops)),
            dma((ops,)),
            dma((ops,)),
            dma((n,)),
            dma((share,)),
            dma,
            dma,
        ],
        compiler_params=pltpu.CompilerParams(
            collective_id=0, has_side_effects=True, vmem_limit_bytes=63 * 1024 * 1024
        ),
        cost_estimate=pl.CostEstimate(
            flops=flops, bytes_accessed=1 << 20, transcendentals=0
        ),
    )(rows_live, cols_live, block_live, states, left_ops, right_ops)
    return pl.pallas_call(
        write_out,
        out_shape=tuple(jax.ShapeDtypeStruct(r.shape, r.dtype) for r in results),
        in_specs=[hbm] * 3,
        out_specs=(hbm,) * 3,
        scratch_shapes=[dma((3,))],
        compiler_params=pltpu.CompilerParams(vmem_limit_bytes=63 * 1024 * 1024),
    )(*results)


def solution(mesh):
    placed = (
        P("groups", "sector", None, None, None),
        P("op", ("groups", "sector"), None, None),
        P("op", ("groups", "sector"), None, None),
        P("groups"),
        P("groups"),
        P("groups", None),
    )
    return jax.shard_map(
        functools.partial(on_device, mesh),
        mesh=mesh,
        in_specs=placed,
        out_specs=(P("groups", "op", "sector", None, None), P("groups", None), P("groups", None)),
        check_vma=False,
    )
```

```python
import functools

import jax
import jax.numpy as jnp
from jax import lax
from jax.experimental import pallas as pl
from jax.experimental.pallas import tpu as pltpu
from jax.sharding import PartitionSpec as P

MESH = pl.DeviceIdType.MESH


def each(count, body):
    if count <= 16:
        for i in range(count):
            body(i)
    else:
        lax.fori_loop(0, count, lambda i, c: (body(i), c)[1], 0)


def kernel(
    n, ops, norm,
    rows_hbm, cols_hbm, blocks_hbm, states_ref, left_ref, right_ref,
    sigma_out, stats,
    sigma_ref, own_sums,
    rows_ref, cols_ref, blocks_ref,
    left_own, left_send_buf, left_all, right_all, states_all,
    local_sem, left_ss, left_rs, right_ss, right_rs, st_ss, st_rs, stat_ss, stat_rs,
):
    s = lax.axis_index("sector")
    o = lax.axis_index("op")
    share = states_all.shape[0]
    kl = left_own.shape[0]
    rows, width = states_all.shape[2:]
    owner = s // share
    slot = lax.rem(s, share)
    mate = o + 1 - 2 * lax.rem(o, 2)

    barrier = pltpu.get_barrier_semaphore()

    def greet(r):
        pl.semaphore_signal(
            barrier,
            inc=1,
            device_id={
                "sector": lax.rem(s + (r + 1) // ops, n),
                "op": lax.rem(o + lax.rem(r + 1, ops), ops),
            },
            device_id_type=MESH,
        )

    each(n * ops - 1, greet)

    load_left = pltpu.make_async_copy(left_ref.at[:, 0], left_own, local_sem.at[0])
    load_left.start()
    load_right = pltpu.make_async_copy(right_ref.at[:, 0], right_all.at[o], local_sem.at[1])
    load_right.start()
    load_states = pltpu.make_async_copy(
        states_ref.at[:, 0, s], states_all.at[slot], local_sem.at[2]
    )

    @pl.when(owner == o)
    def _():
        load_states.start()

    tables = [
        pltpu.make_async_copy(src, dst, local_sem.at[3 + i])
        for i, (src, dst) in enumerate(
            [(rows_hbm, rows_ref), (cols_hbm, cols_ref), (blocks_hbm, blocks_ref)]
        )
    ]
    for copy in tables:
        copy.start()

    load_left.wait()
    packed = [
        jnp.concatenate([left_own[2 * j], left_own[2 * j + 1]], axis=1) for j in range(kl // 2)
    ]
    for j in range(kl // 2):
        left_send_buf[j] = packed[j]

    @pl.when(owner == o)
    def _():
        for j in range(kl // 2):
            left_all[slot, o, j] = packed[j]

    pl.semaphore_wait(barrier, n * ops - 1)

    def right_copy(origin, src, to, sem):
        return pltpu.make_async_remote_copy(
            src_ref=src,
            dst_ref=right_all.at[origin],
            send_sem=right_ss.at[sem],
            recv_sem=right_rs.at[origin],
            device_id={"op": to},
            device_id_type=MESH,
        )

    far = [lax.rem(o + 2 * p, ops) for p in range(1, ops // 2)]
    own_right = right_ref.at[:, 0]
    sends = [right_copy(o, own_right, far[p], p) for p in range(len(far))]
    sends.append(right_copy(o, own_right, mate, len(far)))
    for copy in sends:
        copy.start()

    def left_copy(d):
        return pltpu.make_async_remote_copy(
            src_ref=left_send_buf,
            dst_ref=left_all.at[slot, o],
            send_sem=left_ss.at[d],
            recv_sem=left_rs.at[slot, o],
            device_id={"sector": lax.rem(s + d, n), "op": owner},
            device_id_type=MESH,
        )

    def state_copy(d):
        to = lax.rem(s + d, n)
        return pltpu.make_async_remote_copy(
            src_ref=states_ref.at[:, 0, to],
            dst_ref=states_all.at[slot],
            send_sem=st_ss.at[d],
            recv_sem=st_rs.at[slot],
            device_id={"sector": to, "op": o},
            device_id_type=MESH,
        )

    @pl.when(owner == o)
    def _():
        each(n - 1, lambda d: state_copy(d + 1).start())

    each(n - 1, lambda d: left_copy(d + 1).start())

    @pl.when(owner != o)
    def _():
        left_copy(0).start()

    for p in range(len(far)):
        origin = far[p]
        right_copy(origin, right_all.at[origin], mate, len(far) + 1 + p).wait_recv()
        copy = right_copy(origin, right_all.at[origin], mate, len(far) + 1 + p)
        copy.start()
        sends.append(copy)

    load_right.wait()
    for copy in tables:
        copy.wait()

    @pl.when(owner == o)
    def _():
        load_states.wait()

    row_at = lax.broadcasted_iota(jnp.int32, (rows, width), 0)
    col_at = lax.broadcasted_iota(jnp.int32, (rows, width), 1)
    zero = jnp.zeros((rows, width), jnp.bfloat16)
    totals = [jnp.zeros((1, width), jnp.float32) for _ in range(8)]

    def one_block(i, totals, first):
        a = o * share + i

        @pl.when(a != s)
        def _():
            state_copy_in(i).wait_recv()

        live = (
            (row_at < rows_ref[a]) & (col_at < cols_ref[s]) & (blocks_ref[a, s] == 1)
        )
        masked = [
            jnp.where(live, states_all[i, v].astype(jnp.float32), 0.0) for v in range(2)
        ]
        narrow = [m.astype(jnp.bfloat16) for m in masked]
        pairs = [
            jnp.concatenate(
                [
                    jnp.concatenate([m, zero], axis=1),
                    jnp.concatenate([zero, m], axis=1),
                ],
                axis=0,
            )
            for m in narrow
        ]
        acc = jnp.zeros((2 * rows, width), jnp.float32)
        for step in range(ops):
            if step == 0:
                g = o
            elif step == 1:
                g = mate
            elif step % 2 == 0:
                g = far[step // 2 - 1]
            else:
                f = far[step // 2 - 1]
                g = f + 1 - 2 * lax.rem(f, 2)

            @pl.when(jnp.logical_or(a != s, g != o))
            def _():
                left_copy_in(i, g).wait_recv()

            if first and step % 2 == 1:
                right_copy(g, right_all.at[g], mate, 0).wait_recv()
            lhs = left_all[i, g].reshape(kl // 2 * rows, 2 * rows)
            done = []
            for v in range(2):
                t = jnp.dot(lhs, pairs[v], preferred_element_type=jnp.float32)
                t = t.astype(jnp.bfloat16)
                done.append(
                    jnp.concatenate(
                        [t[j * rows:(j + 1) * rows] for j in range(kl // 2)], axis=1
                    )
                )
            rhs = jnp.concatenate([right_all[g, k] for k in range(kl)], axis=1)
            acc += lax.dot_general(
                jnp.concatenate(done, axis=0), rhs, (((1,), (1,)), ((), ())),
                preferred_element_type=jnp.float32,
            )
        summed = [
            jnp.where(live, acc[v * rows:(v + 1) * rows], 0.0) for v in range(2)
        ]
        for v in range(2):
            sigma_ref[v, i, 0] = summed[v].astype(jnp.bfloat16)
        out = []
        for right in (summed, masked):
            for v in range(2):
                for w in range(2):
                    out.append(jnp.sum(masked[v] * right[w], axis=0, keepdims=True))
        return [x + y for x, y in zip(totals, out)]

    def state_copy_in(i):
        return pltpu.make_async_remote_copy(
            src_ref=states_ref.at[:, 0, s],
            dst_ref=states_all.at[i],
            send_sem=st_ss.at[0],
            recv_sem=st_rs.at[i],
            device_id={"sector": lax.rem(s + 1, n), "op": o},
            device_id_type=MESH,
        )

    def left_copy_in(i, g):
        return pltpu.make_async_remote_copy(
            src_ref=left_send_buf,
            dst_ref=left_all.at[i, g],
            send_sem=left_ss.at[0],
            recv_sem=left_rs.at[i, g],
            device_id={"sector": lax.rem(s + 1, n), "op": o},
            device_id_type=MESH,
        )

    totals = one_block(0, totals, True)
    if share > 1:
        totals = lax.fori_loop(
            1, share, lambda i, t: tuple(one_block(i, list(t), False)), tuple(totals)
        )

    rank = s * ops + o
    outs = [
        pltpu.make_async_copy(sigma_ref, sigma_out, local_sem.at[6]),
        pltpu.make_async_copy(own_sums, stats.at[rank], local_sem.at[7]),
    ]

    sums = jnp.sum(jnp.concatenate(list(totals), axis=0), axis=1, keepdims=True)
    at_row = lax.broadcasted_iota(jnp.int32, (8, width), 0)
    at_lane = lax.broadcasted_iota(jnp.int32, (8, width), 1)
    own_sums[...] = jnp.sum(
        jnp.where(at_row == at_lane, sums * norm, 0.0), axis=0, keepdims=True
    )

    def tell(r):
        pltpu.make_async_remote_copy(
            src_ref=own_sums,
            dst_ref=stats.at[rank],
            send_sem=stat_ss,
            recv_sem=stat_rs,
            device_id={
                "sector": lax.rem(s + (r + 1) // ops, n),
                "op": lax.rem(o + lax.rem(r + 1, ops), ops),
            },
            device_id_type=MESH,
        ).start()

    each(n * ops - 1, tell)
    for copy in outs:
        copy.start()

    for copy in sends:
        copy.wait_send()

    @pl.when(owner == o)
    def _():
        each(n - 1, lambda d: state_copy(d + 1).wait_send())

    each(n - 1, lambda d: left_copy(d + 1).wait_send())

    @pl.when(owner != o)
    def _():
        left_copy(0).wait_send()

    others = stats.at[pl.ds(0, n * ops - 1)]
    both = pltpu.make_async_remote_copy(
        src_ref=others, dst_ref=others, send_sem=stat_ss, recv_sem=stat_rs,
        device_id={"sector": lax.rem(s + 1, n), "op": o}, device_id_type=MESH,
    )
    both.wait_recv()
    both.wait_send()
    for copy in outs:
        copy.wait()


def write_out(
    sigma_in, stats_in, sigma_out, ray_out, corr_out, sigma, stats, ray, corr, in_sem, out_sem
):
    load_sigma = pltpu.make_async_copy(sigma_in, sigma, in_sem.at[0])
    load_stats = pltpu.make_async_copy(stats_in, stats, in_sem.at[1])
    load_stats.start()
    load_sigma.start()
    load_stats.wait()
    result = jnp.sum(stats[...], axis=0)
    for v in range(2):
        ray[v:v + 1, :] = result[:, 2 * v:2 * v + 2]
        corr[v:v + 1, :] = result[:, 4 + 2 * v:6 + 2 * v]
    copies = [
        pltpu.make_async_copy(src, dst, out_sem.at[i])
        for i, (src, dst) in enumerate([(ray, ray_out), (corr, corr_out), (sigma, sigma_out)])
    ]
    copies[0].start()
    copies[1].start()
    load_sigma.wait()
    copies[2].start()
    for copy in copies:
        copy.wait()


def on_device(mesh, states, left_ops, right_ops, rows_live, cols_live, block_live):
    n = mesh.shape["sector"]
    ops = mesh.shape["op"]
    kl, _, rows, _ = left_ops.shape
    width = right_ops.shape[2]
    nv = states.shape[0]
    left_sectors, right_sectors = block_live.shape
    share = left_sectors // ops
    assert nv == 2 and kl % 2 == 0 and ops % 2 == 0
    assert left_ops.shape[1] == 1 and right_ops.shape[1] == 1 and states.shape[1] == 1
    norm = 1.0 / (left_sectors * right_sectors * rows * width)
    hbm = pl.BlockSpec(memory_space=pltpu.HBM)
    dma = pltpu.SemaphoreType.DMA
    flops = 2 * nv * share * ops * kl * rows * width * (rows + width)
    sigma, stats = pl.pallas_call(
        functools.partial(kernel, n, ops, norm),
        out_shape=(
            jax.ShapeDtypeStruct((nv, share, 1, rows, width), jnp.bfloat16),
            jax.ShapeDtypeStruct((n * ops, 1, width), jnp.float32),
        ),
        in_specs=[hbm] * 6,
        out_specs=(hbm,) * 2,
        scratch_shapes=[
            pltpu.VMEM((nv, share, 1, rows, width), jnp.bfloat16),
            pltpu.VMEM((1, width), jnp.float32),
            pltpu.SMEM(rows_live.shape, jnp.int32),
            pltpu.SMEM(cols_live.shape, jnp.int32),
            pltpu.SMEM(block_live.shape, jnp.int32),
            pltpu.VMEM((kl, rows, rows), jnp.bfloat16),
            pltpu.VMEM((kl // 2, rows, 2 * rows), jnp.bfloat16),
            pltpu.VMEM((share, ops, kl // 2, rows, 2 * rows), jnp.bfloat16),
            pltpu.VMEM((ops, kl, width, width), jnp.bfloat16),
            pltpu.VMEM((share, nv, rows, width), jnp.bfloat16),
            dma((8,)),
            dma((n,)),
            dma((share, ops)),
            dma((ops,)),
            dma((ops,)),
            dma((n,)),
            dma((share,)),
            dma,
            dma,
        ],
        compiler_params=pltpu.CompilerParams(
            collective_id=0, has_side_effects=True, vmem_limit_bytes=63 * 1024 * 1024
        ),
        cost_estimate=pl.CostEstimate(
            flops=flops, bytes_accessed=1 << 20, transcendentals=0
        ),
    )(rows_live, cols_live, block_live, states, left_ops, right_ops)
    return pl.pallas_call(
        write_out,
        out_shape=(
            jax.ShapeDtypeStruct(sigma.shape, sigma.dtype),
            jax.ShapeDtypeStruct((nv, nv), jnp.float32),
            jax.ShapeDtypeStruct((nv, nv), jnp.float32),
        ),
        in_specs=[hbm] * 2,
        out_specs=(hbm,) * 3,
        scratch_shapes=[
            pltpu.VMEM(sigma.shape, sigma.dtype),
            pltpu.VMEM(stats.shape, stats.dtype),
            pltpu.VMEM((nv, nv), jnp.float32),
            pltpu.VMEM((nv, nv), jnp.float32),
            dma((2,)),
            dma((3,)),
        ],
        compiler_params=pltpu.CompilerParams(vmem_limit_bytes=63 * 1024 * 1024),
    )(sigma, stats)


def solution(mesh):
    placed = (
        P("groups", "sector", None, None, None),
        P("op", ("groups", "sector"), None, None),
        P("op", ("groups", "sector"), None, None),
        P("groups"),
        P("groups"),
        P("groups", None),
    )
    return jax.shard_map(
        functools.partial(on_device, mesh),
        mesh=mesh,
        in_specs=placed,
        out_specs=(P("groups", "op", "sector", None, None), P("groups", None), P("groups", None)),
        check_vma=False,
    )
```

```python
import functools

import jax
import jax.numpy as jnp
from jax import lax
from jax.experimental import pallas as pl
from jax.experimental.pallas import tpu as pltpu
from jax.sharding import PartitionSpec as P

MESH = pl.DeviceIdType.MESH


def each(count, body):
    if count <= 16:
        for i in range(count):
            body(i)
    else:
        lax.fori_loop(0, count, lambda i, c: (body(i), c)[1], 0)


def kernel(
    n, ops, norm,
    rows_hbm, cols_hbm, blocks_hbm, states_ref, left_ref, right_ref,
    sigma_out, stats,
    sigma_ref, own_sums,
    rows_ref, cols_ref, blocks_ref,
    left_own, left_send_buf, left_all, right_all, states_all,
    local_sem, left_ss, left_rs, right_ss, right_rs, st_ss, st_rs, stat_ss, stat_rs,
):
    s = lax.axis_index("sector")
    o = lax.axis_index("op")
    share = states_all.shape[0]
    kl = left_own.shape[0]
    rows, width = states_all.shape[2:]
    owner = s // share
    slot = lax.rem(s, share)
    mate = o + 1 - 2 * lax.rem(o, 2)

    barrier = pltpu.get_barrier_semaphore()

    def greet(r):
        pl.semaphore_signal(
            barrier,
            inc=1,
            device_id={
                "sector": lax.rem(s + (r + 1) // ops, n),
                "op": lax.rem(o + lax.rem(r + 1, ops), ops),
            },
            device_id_type=MESH,
        )

    each(n * ops - 1, greet)

    load_left = pltpu.make_async_copy(left_ref.at[:, 0], left_own, local_sem.at[0])
    load_left.start()
    load_right = pltpu.make_async_copy(right_ref.at[:, 0], right_all.at[o], local_sem.at[1])
    load_right.start()
    load_states = pltpu.make_async_copy(
        states_ref.at[:, 0, s], states_all.at[slot], local_sem.at[2]
    )

    @pl.when(owner == o)
    def _():
        load_states.start()

    tables = [
        pltpu.make_async_copy(src, dst, local_sem.at[3 + i])
        for i, (src, dst) in enumerate(
            [(rows_hbm, rows_ref), (cols_hbm, cols_ref), (blocks_hbm, blocks_ref)]
        )
    ]
    for copy in tables:
        copy.start()

    load_left.wait()
    packed = [
        jnp.concatenate([left_own[2 * j], left_own[2 * j + 1]], axis=1) for j in range(kl // 2)
    ]
    for j in range(kl // 2):
        left_send_buf[j] = packed[j]

    @pl.when(owner == o)
    def _():
        for j in range(kl // 2):
            left_all[slot, o, j] = packed[j]

    pl.semaphore_wait(barrier, n * ops - 1)

    def right_copy(origin, src, to, sem):
        return pltpu.make_async_remote_copy(
            src_ref=src,
            dst_ref=right_all.at[origin],
            send_sem=right_ss.at[sem],
            recv_sem=right_rs.at[origin],
            device_id={"op": to},
            device_id_type=MESH,
        )

    far = [lax.rem(o + 2 * p, ops) for p in range(1, ops // 2)]
    own_right = right_ref.at[:, 0]
    sends = [right_copy(o, own_right, far[p], p) for p in range(len(far))]
    sends.append(right_copy(o, own_right, mate, len(far)))
    for copy in sends:
        copy.start()

    def left_copy(d):
        return pltpu.make_async_remote_copy(
            src_ref=left_send_buf,
            dst_ref=left_all.at[slot, o],
            send_sem=left_ss.at[d],
            recv_sem=left_rs.at[slot, o],
            device_id={"sector": lax.rem(s + d, n), "op": owner},
            device_id_type=MESH,
        )

    def state_copy(d):
        to = lax.rem(s + d, n)
        return pltpu.make_async_remote_copy(
            src_ref=states_ref.at[:, 0, to],
            dst_ref=states_all.at[slot],
            send_sem=st_ss.at[d],
            recv_sem=st_rs.at[slot],
            device_id={"sector": to, "op": o},
            device_id_type=MESH,
        )

    @pl.when(owner == o)
    def _():
        each(n - 1, lambda d: state_copy(d + 1).start())

    each(n - 1, lambda d: left_copy(d + 1).start())

    @pl.when(owner != o)
    def _():
        left_copy(0).start()

    for p in range(len(far)):
        origin = far[p]
        right_copy(origin, right_all.at[origin], mate, len(far) + 1 + p).wait_recv()
        copy = right_copy(origin, right_all.at[origin], mate, len(far) + 1 + p)
        copy.start()
        sends.append(copy)

    load_right.wait()
    for copy in tables:
        copy.wait()

    @pl.when(owner == o)
    def _():
        load_states.wait()

    row_at = lax.broadcasted_iota(jnp.int32, (rows, width), 0)
    col_at = lax.broadcasted_iota(jnp.int32, (rows, width), 1)
    zero = jnp.zeros((rows, width), jnp.bfloat16)
    totals = [jnp.zeros((1, width), jnp.float32) for _ in range(8)]

    def one_block(i, totals, first):
        a = o * share + i

        @pl.when(a != s)
        def _():
            state_copy_in(i).wait_recv()

        live = (
            (row_at < rows_ref[a]) & (col_at < cols_ref[s]) & (blocks_ref[a, s] == 1)
        )
        masked = [
            jnp.where(live, states_all[i, v].astype(jnp.float32), 0.0) for v in range(2)
        ]
        narrow = [m.astype(jnp.bfloat16) for m in masked]
        pairs = [
            jnp.concatenate(
                [
                    jnp.concatenate([m, zero], axis=1),
                    jnp.concatenate([zero, m], axis=1),
                ],
                axis=0,
            )
            for m in narrow
        ]

        def products(right):
            return [
                jnp.sum(masked[v] * right[w], axis=0, keepdims=True)
                for v in range(2)
                for w in range(2)
            ]

        overlaps = products(masked)
        acc = jnp.zeros((2 * rows, width), jnp.float32)
        for step in range(ops):
            if step == 0:
                g = o
            elif step == 1:
                g = mate
            elif step % 2 == 0:
                g = far[step // 2 - 1]
            else:
                f = far[step // 2 - 1]
                g = f + 1 - 2 * lax.rem(f, 2)

            @pl.when(jnp.logical_or(a != s, g != o))
            def _():
                left_copy_in(i, g).wait_recv()

            if first and step % 2 == 1:
                right_copy(g, right_all.at[g], mate, 0).wait_recv()
            lhs = left_all[i, g].reshape(kl // 2 * rows, 2 * rows)
            done = []
            for v in range(2):
                t = jnp.dot(lhs, pairs[v], preferred_element_type=jnp.float32)
                t = t.astype(jnp.bfloat16)
                done.append(
                    jnp.concatenate(
                        [t[j * rows:(j + 1) * rows] for j in range(kl // 2)], axis=1
                    )
                )
            rhs = jnp.concatenate([right_all[g, k] for k in range(kl)], axis=1)
            acc += lax.dot_general(
                jnp.concatenate(done, axis=0), rhs, (((1,), (1,)), ((), ())),
                preferred_element_type=jnp.float32,
            )
        summed = [
            jnp.where(live, acc[v * rows:(v + 1) * rows], 0.0) for v in range(2)
        ]
        for v in range(2):
            sigma_ref[v, i, 0] = summed[v].astype(jnp.bfloat16)
        out = products(summed) + overlaps
        return [x + y for x, y in zip(totals, out)]

    def state_copy_in(i):
        return pltpu.make_async_remote_copy(
            src_ref=states_ref.at[:, 0, s],
            dst_ref=states_all.at[i],
            send_sem=st_ss.at[0],
            recv_sem=st_rs.at[i],
            device_id={"sector": lax.rem(s + 1, n), "op": o},
            device_id_type=MESH,
        )

    def left_copy_in(i, g):
        return pltpu.make_async_remote_copy(
            src_ref=left_send_buf,
            dst_ref=left_all.at[i, g],
            send_sem=left_ss.at[0],
            recv_sem=left_rs.at[i, g],
            device_id={"sector": lax.rem(s + 1, n), "op": o},
            device_id_type=MESH,
        )

    totals = one_block(0, totals, True)
    if share > 1:
        totals = lax.fori_loop(
            1, share, lambda i, t: tuple(one_block(i, list(t), False)), tuple(totals)
        )

    rank = s * ops + o
    outs = [
        pltpu.make_async_copy(sigma_ref, sigma_out, local_sem.at[6]),
        pltpu.make_async_copy(own_sums, stats.at[rank], local_sem.at[7]),
    ]

    sums = jnp.sum(jnp.concatenate(list(totals), axis=0), axis=1, keepdims=True)
    at_row = lax.broadcasted_iota(jnp.int32, (8, width), 0)
    at_lane = lax.broadcasted_iota(jnp.int32, (8, width), 1)
    own_sums[...] = jnp.sum(
        jnp.where(at_row == at_lane, sums * norm, 0.0), axis=0, keepdims=True
    )

    def tell(r):
        pltpu.make_async_remote_copy(
            src_ref=own_sums,
            dst_ref=stats.at[rank],
            send_sem=stat_ss,
            recv_sem=stat_rs,
            device_id={
                "sector": lax.rem(s + (r + 1) // ops, n),
                "op": lax.rem(o + lax.rem(r + 1, ops), ops),
            },
            device_id_type=MESH,
        ).start()

    each(n * ops - 1, tell)
    for copy in outs:
        copy.start()

    for copy in sends:
        copy.wait_send()

    @pl.when(owner == o)
    def _():
        each(n - 1, lambda d: state_copy(d + 1).wait_send())

    each(n - 1, lambda d: left_copy(d + 1).wait_send())

    @pl.when(owner != o)
    def _():
        left_copy(0).wait_send()

    others = stats.at[pl.ds(0, n * ops - 1)]
    both = pltpu.make_async_remote_copy(
        src_ref=others, dst_ref=others, send_sem=stat_ss, recv_sem=stat_rs,
        device_id={"sector": lax.rem(s + 1, n), "op": o}, device_id_type=MESH,
    )
    both.wait_recv()
    both.wait_send()
    for copy in outs:
        copy.wait()


def write_out(
    sigma_in, stats_in, sigma_out, ray_out, corr_out, sigma, stats, ray, corr, in_sem, out_sem
):
    load_sigma = pltpu.make_async_copy(sigma_in, sigma, in_sem.at[0])
    load_stats = pltpu.make_async_copy(stats_in, stats, in_sem.at[1])
    load_stats.start()
    load_sigma.start()
    load_stats.wait()
    result = jnp.sum(stats[...], axis=0)
    for v in range(2):
        ray[v:v + 1, :] = result[:, 2 * v:2 * v + 2]
        corr[v:v + 1, :] = result[:, 4 + 2 * v:6 + 2 * v]
    copies = [
        pltpu.make_async_copy(src, dst, out_sem.at[i])
        for i, (src, dst) in enumerate([(ray, ray_out), (corr, corr_out), (sigma, sigma_out)])
    ]
    copies[0].start()
    copies[1].start()
    load_sigma.wait()
    copies[2].start()
    for copy in copies:
        copy.wait()


def on_device(mesh, states, left_ops, right_ops, rows_live, cols_live, block_live):
    n = mesh.shape["sector"]
    ops = mesh.shape["op"]
    kl, _, rows, _ = left_ops.shape
    width = right_ops.shape[2]
    nv = states.shape[0]
    left_sectors, right_sectors = block_live.shape
    share = left_sectors // ops
    assert nv == 2 and kl % 2 == 0 and ops % 2 == 0
    assert left_ops.shape[1] == 1 and right_ops.shape[1] == 1 and states.shape[1] == 1
    norm = 1.0 / (left_sectors * right_sectors * rows * width)
    hbm = pl.BlockSpec(memory_space=pltpu.HBM)
    dma = pltpu.SemaphoreType.DMA
    flops = 2 * nv * share * ops * kl * rows * width * (rows + width)
    sigma, stats = pl.pallas_call(
        functools.partial(kernel, n, ops, norm),
        out_shape=(
            jax.ShapeDtypeStruct((nv, share, 1, rows, width), jnp.bfloat16),
            jax.ShapeDtypeStruct((n * ops, 1, width), jnp.float32),
        ),
        in_specs=[hbm] * 6,
        out_specs=(hbm,) * 2,
        scratch_shapes=[
            pltpu.VMEM((nv, share, 1, rows, width), jnp.bfloat16),
            pltpu.VMEM((1, width), jnp.float32),
            pltpu.SMEM(rows_live.shape, jnp.int32),
            pltpu.SMEM(cols_live.shape, jnp.int32),
            pltpu.SMEM(block_live.shape, jnp.int32),
            pltpu.VMEM((kl, rows, rows), jnp.bfloat16),
            pltpu.VMEM((kl // 2, rows, 2 * rows), jnp.bfloat16),
            pltpu.VMEM((share, ops, kl // 2, rows, 2 * rows), jnp.bfloat16),
            pltpu.VMEM((ops, kl, width, width), jnp.bfloat16),
            pltpu.VMEM((share, nv, rows, width), jnp.bfloat16),
            dma((8,)),
            dma((n,)),
            dma((share, ops)),
            dma((ops,)),
            dma((ops,)),
            dma((n,)),
            dma((share,)),
            dma,
            dma,
        ],
        compiler_params=pltpu.CompilerParams(
            collective_id=0, has_side_effects=True, vmem_limit_bytes=63 * 1024 * 1024
        ),
        cost_estimate=pl.CostEstimate(
            flops=flops, bytes_accessed=1 << 20, transcendentals=0
        ),
    )(rows_live, cols_live, block_live, states, left_ops, right_ops)
    return pl.pallas_call(
        write_out,
        out_shape=(
            jax.ShapeDtypeStruct(sigma.shape, sigma.dtype),
            jax.ShapeDtypeStruct((nv, nv), jnp.float32),
            jax.ShapeDtypeStruct((nv, nv), jnp.float32),
        ),
        in_specs=[hbm] * 2,
        out_specs=(hbm,) * 3,
        scratch_shapes=[
            pltpu.VMEM(sigma.shape, sigma.dtype),
            pltpu.VMEM(stats.shape, stats.dtype),
            pltpu.VMEM((nv, nv), jnp.float32),
            pltpu.VMEM((nv, nv), jnp.float32),
            dma((2,)),
            dma((3,)),
        ],
        compiler_params=pltpu.CompilerParams(vmem_limit_bytes=63 * 1024 * 1024),
    )(sigma, stats)


def solution(mesh):
    placed = (
        P("groups", "sector", None, None, None),
        P("op", ("groups", "sector"), None, None),
        P("op", ("groups", "sector"), None, None),
        P("groups"),
        P("groups"),
        P("groups", None),
    )
    return jax.shard_map(
        functools.partial(on_device, mesh),
        mesh=mesh,
        in_specs=placed,
        out_specs=(P("groups", "op", "sector", None, None), P("groups", None), P("groups", None)),
        check_vma=False,
    )
```

```python
import functools

import jax
import jax.numpy as jnp
from jax import lax
from jax.experimental import pallas as pl
from jax.experimental.pallas import tpu as pltpu
from jax.sharding import PartitionSpec as P

MESH = pl.DeviceIdType.MESH


def each(count, body):
    if count <= 16:
        for i in range(count):
            body(i)
    else:
        lax.fori_loop(0, count, lambda i, c: (body(i), c)[1], 0)


def kernel(
    n, ops, norm,
    rows_hbm, cols_hbm, blocks_hbm, states_ref, left_ref, right_ref,
    sigma_out, stats,
    sigma_ref, own_sums,
    rows_ref, cols_ref, blocks_ref,
    left_own, left_send_buf, left_all, right_all, states_all,
    local_sem, left_ss, left_rs, right_ss, right_rs, st_ss, st_rs, stat_ss, stat_rs,
):
    s = lax.axis_index("sector")
    o = lax.axis_index("op")
    share = states_all.shape[0]
    kl = left_own.shape[0]
    rows, width = states_all.shape[2:]
    owner = s // share
    slot = lax.rem(s, share)
    mate = o + 1 - 2 * lax.rem(o, 2)

    barrier = pltpu.get_barrier_semaphore()

    def greet(r):
        pl.semaphore_signal(
            barrier,
            inc=1,
            device_id={
                "sector": lax.rem(s + (r + 1) // ops, n),
                "op": lax.rem(o + lax.rem(r + 1, ops), ops),
            },
            device_id_type=MESH,
        )

    each(n * ops - 1, lambda r: greet(n * ops - 2 - r))

    load_left = pltpu.make_async_copy(left_ref.at[:, 0], left_own, local_sem.at[0])
    load_left.start()
    load_right = pltpu.make_async_copy(right_ref.at[:, 0], right_all.at[o], local_sem.at[1])
    load_right.start()
    load_states = pltpu.make_async_copy(
        states_ref.at[:, 0, s], states_all.at[slot], local_sem.at[2]
    )

    @pl.when(owner == o)
    def _():
        load_states.start()

    tables = [
        pltpu.make_async_copy(src, dst, local_sem.at[3 + i])
        for i, (src, dst) in enumerate(
            [(rows_hbm, rows_ref), (cols_hbm, cols_ref), (blocks_hbm, blocks_ref)]
        )
    ]
    for copy in tables:
        copy.start()

    load_left.wait()
    packed = [
        jnp.concatenate([left_own[2 * j], left_own[2 * j + 1]], axis=1) for j in range(kl // 2)
    ]
    for j in range(kl // 2):
        left_send_buf[j] = packed[j]

    @pl.when(owner == o)
    def _():
        for j in range(kl // 2):
            left_all[slot, o, j] = packed[j]

    pl.semaphore_wait(barrier, n * ops - 1)

    def right_copy(origin, src, to, sem):
        return pltpu.make_async_remote_copy(
            src_ref=src,
            dst_ref=right_all.at[origin],
            send_sem=right_ss.at[sem],
            recv_sem=right_rs.at[origin],
            device_id={"op": to},
            device_id_type=MESH,
        )

    far = [lax.rem(o + 2 * p, ops) for p in range(1, ops // 2)]
    own_right = right_ref.at[:, 0]
    sends = [right_copy(o, own_right, far[p], p) for p in range(len(far))]
    sends.append(right_copy(o, own_right, mate, len(far)))
    for copy in sends:
        copy.start()

    def left_copy(d):
        return pltpu.make_async_remote_copy(
            src_ref=left_send_buf,
            dst_ref=left_all.at[slot, o],
            send_sem=left_ss.at[d],
            recv_sem=left_rs.at[slot, o],
            device_id={"sector": lax.rem(s + d, n), "op": owner},
            device_id_type=MESH,
        )

    def state_copy(d):
        to = lax.rem(s + d, n)
        return pltpu.make_async_remote_copy(
            src_ref=states_ref.at[:, 0, to],
            dst_ref=states_all.at[slot],
            send_sem=st_ss.at[d],
            recv_sem=st_rs.at[slot],
            device_id={"sector": to, "op": o},
            device_id_type=MESH,
        )

    @pl.when(owner == o)
    def _():
        each(n - 1, lambda d: state_copy(d + 1).start())

    each(n - 1, lambda d: left_copy(d + 1).start())

    @pl.when(owner != o)
    def _():
        left_copy(0).start()

    for p in range(len(far)):
        origin = far[p]
        right_copy(origin, right_all.at[origin], mate, len(far) + 1 + p).wait_recv()
        copy = right_copy(origin, right_all.at[origin], mate, len(far) + 1 + p)
        copy.start()
        sends.append(copy)

    load_right.wait()
    for copy in tables:
        copy.wait()

    @pl.when(owner == o)
    def _():
        load_states.wait()

    row_at = lax.broadcasted_iota(jnp.int32, (rows, width), 0)
    col_at = lax.broadcasted_iota(jnp.int32, (rows, width), 1)
    zero = jnp.zeros((rows, width), jnp.bfloat16)
    totals = [jnp.zeros((1, width), jnp.float32) for _ in range(8)]

    def one_block(i, totals, first):
        a = o * share + i

        @pl.when(a != s)
        def _():
            state_copy_in(i).wait_recv()

        live = (
            (row_at < rows_ref[a]) & (col_at < cols_ref[s]) & (blocks_ref[a, s] == 1)
        )
        masked = [
            jnp.where(live, states_all[i, v].astype(jnp.float32), 0.0) for v in range(2)
        ]
        narrow = [m.astype(jnp.bfloat16) for m in masked]
        pairs = [
            jnp.concatenate(
                [
                    jnp.concatenate([m, zero], axis=1),
                    jnp.concatenate([zero, m], axis=1),
                ],
                axis=0,
            )
            for m in narrow
        ]
        acc = jnp.zeros((2 * rows, width), jnp.float32)
        for step in range(ops):
            if step == 0:
                g = o
            elif step == 1:
                g = mate
            elif step % 2 == 0:
                g = far[step // 2 - 1]
            else:
                f = far[step // 2 - 1]
                g = f + 1 - 2 * lax.rem(f, 2)

            @pl.when(jnp.logical_or(a != s, g != o))
            def _():
                left_copy_in(i, g).wait_recv()

            if first and step % 2 == 1:
                right_copy(g, right_all.at[g], mate, 0).wait_recv()
            lhs = left_all[i, g].reshape(kl // 2 * rows, 2 * rows)
            done = []
            for v in range(2):
                t = jnp.dot(lhs, pairs[v], preferred_element_type=jnp.float32)
                t = t.astype(jnp.bfloat16)
                done.append(
                    jnp.concatenate(
                        [t[j * rows:(j + 1) * rows] for j in range(kl // 2)], axis=1
                    )
                )
            rhs = jnp.concatenate([right_all[g, k] for k in range(kl)], axis=1)
            acc += lax.dot_general(
                jnp.concatenate(done, axis=0), rhs, (((1,), (1,)), ((), ())),
                preferred_element_type=jnp.float32,
            )
        summed = [
            jnp.where(live, acc[v * rows:(v + 1) * rows], 0.0) for v in range(2)
        ]
        for v in range(2):
            sigma_ref[v, i, 0] = summed[v].astype(jnp.bfloat16)
        out = []
        for right in (summed, masked):
            for v in range(2):
                for w in range(2):
                    out.append(jnp.sum(masked[v] * right[w], axis=0, keepdims=True))
        return [x + y for x, y in zip(totals, out)]

    def state_copy_in(i):
        return pltpu.make_async_remote_copy(
            src_ref=states_ref.at[:, 0, s],
            dst_ref=states_all.at[i],
            send_sem=st_ss.at[0],
            recv_sem=st_rs.at[i],
            device_id={"sector": lax.rem(s + 1, n), "op": o},
            device_id_type=MESH,
        )

    def left_copy_in(i, g):
        return pltpu.make_async_remote_copy(
            src_ref=left_send_buf,
            dst_ref=left_all.at[i, g],
            send_sem=left_ss.at[0],
            recv_sem=left_rs.at[i, g],
            device_id={"sector": lax.rem(s + 1, n), "op": o},
            device_id_type=MESH,
        )

    totals = one_block(0, totals, True)
    if share > 1:
        totals = lax.fori_loop(
            1, share, lambda i, t: tuple(one_block(i, list(t), False)), tuple(totals)
        )

    rank = s * ops + o
    outs = [
        pltpu.make_async_copy(sigma_ref, sigma_out, local_sem.at[6]),
        pltpu.make_async_copy(own_sums, stats.at[rank], local_sem.at[7]),
    ]

    sums = jnp.sum(jnp.concatenate(list(totals), axis=0), axis=1, keepdims=True)
    at_row = lax.broadcasted_iota(jnp.int32, (8, width), 0)
    at_lane = lax.broadcasted_iota(jnp.int32, (8, width), 1)
    own_sums[...] = jnp.sum(
        jnp.where(at_row == at_lane, sums * norm, 0.0), axis=0, keepdims=True
    )

    def tell(r):
        pltpu.make_async_remote_copy(
            src_ref=own_sums,
            dst_ref=stats.at[rank],
            send_sem=stat_ss,
            recv_sem=stat_rs,
            device_id={
                "sector": lax.rem(s + (r + 1) // ops, n),
                "op": lax.rem(o + lax.rem(r + 1, ops), ops),
            },
            device_id_type=MESH,
        ).start()

    each(n * ops - 1, lambda r: tell(n * ops - 2 - r))
    for copy in outs:
        copy.start()

    for copy in sends:
        copy.wait_send()

    @pl.when(owner == o)
    def _():
        each(n - 1, lambda d: state_copy(d + 1).wait_send())

    each(n - 1, lambda d: left_copy(d + 1).wait_send())

    @pl.when(owner != o)
    def _():
        left_copy(0).wait_send()

    others = stats.at[pl.ds(0, n * ops - 1)]
    both = pltpu.make_async_remote_copy(
        src_ref=others, dst_ref=others, send_sem=stat_ss, recv_sem=stat_rs,
        device_id={"sector": lax.rem(s + 1, n), "op": o}, device_id_type=MESH,
    )
    both.wait_recv()
    both.wait_send()
    for copy in outs:
        copy.wait()


def write_out(
    sigma_in, stats_in, sigma_out, ray_out, corr_out, sigma, stats, ray, corr, in_sem, out_sem
):
    load_sigma = pltpu.make_async_copy(sigma_in, sigma, in_sem.at[0])
    load_stats = pltpu.make_async_copy(stats_in, stats, in_sem.at[1])
    load_stats.start()
    load_sigma.start()
    load_stats.wait()
    result = jnp.sum(stats[...], axis=0)
    for v in range(2):
        ray[v:v + 1, :] = result[:, 2 * v:2 * v + 2]
        corr[v:v + 1, :] = result[:, 4 + 2 * v:6 + 2 * v]
    copies = [
        pltpu.make_async_copy(src, dst, out_sem.at[i])
        for i, (src, dst) in enumerate([(ray, ray_out), (corr, corr_out), (sigma, sigma_out)])
    ]
    copies[0].start()
    copies[1].start()
    load_sigma.wait()
    copies[2].start()
    for copy in copies:
        copy.wait()


def on_device(mesh, states, left_ops, right_ops, rows_live, cols_live, block_live):
    n = mesh.shape["sector"]
    ops = mesh.shape["op"]
    kl, _, rows, _ = left_ops.shape
    width = right_ops.shape[2]
    nv = states.shape[0]
    left_sectors, right_sectors = block_live.shape
    share = left_sectors // ops
    assert nv == 2 and kl % 2 == 0 and ops % 2 == 0
    assert left_ops.shape[1] == 1 and right_ops.shape[1] == 1 and states.shape[1] == 1
    norm = 1.0 / (left_sectors * right_sectors * rows * width)
    hbm = pl.BlockSpec(memory_space=pltpu.HBM)
    dma = pltpu.SemaphoreType.DMA
    flops = 2 * nv * share * ops * kl * rows * width * (rows + width)
    sigma, stats = pl.pallas_call(
        functools.partial(kernel, n, ops, norm),
        out_shape=(
            jax.ShapeDtypeStruct((nv, share, 1, rows, width), jnp.bfloat16),
            jax.ShapeDtypeStruct((n * ops, 1, width), jnp.float32),
        ),
        in_specs=[hbm] * 6,
        out_specs=(hbm,) * 2,
        scratch_shapes=[
            pltpu.VMEM((nv, share, 1, rows, width), jnp.bfloat16),
            pltpu.VMEM((1, width), jnp.float32),
            pltpu.SMEM(rows_live.shape, jnp.int32),
            pltpu.SMEM(cols_live.shape, jnp.int32),
            pltpu.SMEM(block_live.shape, jnp.int32),
            pltpu.VMEM((kl, rows, rows), jnp.bfloat16),
            pltpu.VMEM((kl // 2, rows, 2 * rows), jnp.bfloat16),
            pltpu.VMEM((share, ops, kl // 2, rows, 2 * rows), jnp.bfloat16),
            pltpu.VMEM((ops, kl, width, width), jnp.bfloat16),
            pltpu.VMEM((share, nv, rows, width), jnp.bfloat16),
            dma((8,)),
            dma((n,)),
            dma((share, ops)),
            dma((ops,)),
            dma((ops,)),
            dma((n,)),
            dma((share,)),
            dma,
            dma,
        ],
        compiler_params=pltpu.CompilerParams(
            collective_id=0, has_side_effects=True, vmem_limit_bytes=63 * 1024 * 1024
        ),
        cost_estimate=pl.CostEstimate(
            flops=flops, bytes_accessed=1 << 20, transcendentals=0
        ),
    )(rows_live, cols_live, block_live, states, left_ops, right_ops)
    return pl.pallas_call(
        write_out,
        out_shape=(
            jax.ShapeDtypeStruct(sigma.shape, sigma.dtype),
            jax.ShapeDtypeStruct((nv, nv), jnp.float32),
            jax.ShapeDtypeStruct((nv, nv), jnp.float32),
        ),
        in_specs=[hbm] * 2,
        out_specs=(hbm,) * 3,
        scratch_shapes=[
            pltpu.VMEM(sigma.shape, sigma.dtype),
            pltpu.VMEM(stats.shape, stats.dtype),
            pltpu.VMEM((nv, nv), jnp.float32),
            pltpu.VMEM((nv, nv), jnp.float32),
            dma((2,)),
            dma((3,)),
        ],
        compiler_params=pltpu.CompilerParams(vmem_limit_bytes=63 * 1024 * 1024),
    )(sigma, stats)


def solution(mesh):
    placed = (
        P("groups", "sector", None, None, None),
        P("op", ("groups", "sector"), None, None),
        P("op", ("groups", "sector"), None, None),
        P("groups"),
        P("groups"),
        P("groups", None),
    )
    return jax.shard_map(
        functools.partial(on_device, mesh),
        mesh=mesh,
        in_specs=placed,
        out_specs=(P("groups", "op", "sector", None, None), P("groups", None), P("groups", None)),
        check_vma=False,
    )
```
